128 devices in a mesh: space: 16 (over z, x), tm: 8 (over y, core).
Axes of the slice: x: 4, y: 4, z: 4, core: 2. Of those that a mesh axis runs over, the one named last changes fastest.
Arguments:
- slab: bfloat16 [4096, 128, 1024], P('space', None, 'tm'), may hold values from -22 to 22, as said below
- counts: int32 [4096], replicated, may hold values from 0 to 128
- owner: int32 [4096, 1], replicated, may hold values from 0 to 15; in each aligned block of 256 rows (0 to 255, 256 to 511, ...) at most 24 rows name the same one
- omega: bfloat16 [1024, 128], P('tm'), may hold values from -0.1875 to 0.1875
Outputs:
- probe_owned: bfloat16 [6144, 128, 128], P('space')
- projected: float32 [1024, 128], P('tm')
The draws below stay inside these ranges and needn't reach their ends.
Inputs may be any that keep to these rules, and one draw needn't show every extreme that they name: Within each aligned block of 256 tiles no owner is named more than 24 times, a bound that some block reaches. `slab`: finite field values.
All inputs are finite; a program needn't handle non-finite values.
Results may differ from the reference program's by a relative error of at most 0.025.
Values may be sent and summed in bfloat16 or wider, within the bound.
A program may use at most 128 MiB of HBM per device.

```python
import math
import jax
import jax.numpy as jnp
import numpy as np
from jax import lax

TIME = 1024
K = 128
TILE = 128
TPD = 256
CAP = 24
TILES = 4096
SLOTS = 6144
N_SPACE = 16
N_TM = 8


def draw_slab(key, part):
    key = jax.random.fold_in(key, 1)
    first, second, third = jax.random.split(key, 3)
    offset = jax.random.uniform(first, (TILES, TILE, 1), jnp.float32, -3.0, 3.0)
    spread = jnp.exp(jax.random.uniform(second, (TILES, TILE, 1), jnp.float32, jnp.log(0.3), jnp.log(3.0)))
    noise = jnp.clip(jax.random.normal(third, (TILES, TILE, TIME), jnp.float32), -6.0, 6.0)
    values = offset + spread * noise
    return values.astype(jnp.bfloat16)


def with_ends(result, own_key, smallest, top_value):
    longest = result.shape.index(max(result.shape))
    spots = []
    for shift in (0, 1):
        where = [jax.random.randint(jax.random.fold_in(own_key, axis), (), 0, length) for axis, length in enumerate(result.shape)]
        where[longest] = (where[longest] + shift) % result.shape[longest]
        spots.append(tuple(where))
    return result.at[spots[0]].set(smallest).at[spots[1]].set(top_value)


def steps_of(own_key, extent, shards, least, high):
    def one(position, shards_of):
        heights = jax.random.uniform(jax.random.fold_in(jax.random.fold_in(own_key, 6), position), (shards_of,), jnp.float32, least / len(shards), high / len(shards))
        return jnp.repeat(jnp.exp(heights), extent[position] // shards_of).reshape((-1,) + (1,) * (len(extent) - position - 1))

    level = one(*shards[0])
    for cut in shards[1:]:
        level = level * one(*cut)
    return level


def deal_out(key, own, number, rows, count, top, bound, lean):
    ranking = jax.random.permutation(key, count)
    crowded, ordinary = shares(count, rows * top, bound, lean, True), shares(count, rows * top, bound, lean, False)
    places = jnp.arange(count)

    def named(tallies, offset_by):
        used = int((tallies > 0).sum())
        fixed = max(1, used // 4)
        passed = fixed + (places - fixed + offset_by * (used - fixed)) % max(1, count - fixed)
        return jnp.zeros((count,), jnp.int32).at[ranking[jnp.where(places < fixed, places, passed)]].set(jnp.asarray(tallies, jnp.int32))

    tallies = jnp.where(number % 4 == 0, named(crowded, number // 4), named(ordinary, number - number // 4 - 1))
    mixed = jax.random.permutation(jax.random.fold_in(own, 3), count)
    giver, taker = mixed[0:count // 2 * 2:2], mixed[1:count // 2 * 2:2]
    room = jnp.minimum(tallies[giver] - 1, bound - tallies[taker]) // 2
    room = jnp.where((giver == ranking[0]) | (taker == ranking[0]) | (tallies[taker] == 0), 0, jnp.maximum(room, 0))
    passed = jax.random.randint(jax.random.fold_in(own, 4), (count // 2,), 0, 1 << 20) % (room + 1)
    tallies = tallies.at[giver].add(-passed).at[taker].add(passed)
    labels = jnp.searchsorted(jnp.cumsum(tallies), jnp.arange(rows * top), side="right").astype(jnp.int32)
    listing = labels.reshape(top, rows).T
    listing = listing[jax.random.permutation(jax.random.fold_in(own, 1), rows)]
    offset_by = jax.random.randint(jax.random.fold_in(own, 2), (rows, 1), 0, top)
    return jnp.take_along_axis(listing, (jnp.arange(top)[None, :] + offset_by) % top, axis=1)


def shares(number_of, total, most, skew, full):
    weights = [(1 << 20) // math.isqrt(grade ** skew) + 1 for grade in range(1, number_of + 1)]
    largest = most if full else min(most, max(-(-total // number_of), total * weights[0] // sum(weights)))
    least = 1 if total - largest >= number_of - 1 else 0
    given, surplus = [largest] + [least] * (number_of - 1), total - largest - least * (number_of - 1)
    while surplus > 0:
        candidates = [i for i in range(1, number_of) if given[i] < largest] or [i for i in range(1, number_of) if given[i] < most]
        whole, remaining = sum([weights[i] for i in candidates]), surplus
        for i in candidates:
            addition = min(most - given[i], max(1, remaining * weights[i] // whole), surplus)
            given[i] = given[i] + addition
            surplus = surplus - addition
    return np.array(given)


def normal_values(key, shape, width, most, cuts=(), held_as=jnp.bfloat16):
    values = width * jax.random.normal(key, shape, jnp.float32)
    if cuts:
        values = values * steps_of(key, shape, cuts, -0.22, 0.18)
    return jnp.clip(values, -most, most).astype(held_as)


def setup_inputs(seed: int = 0) -> dict:
    key_of = jax.random.split(jax.random.key(seed), 5)
    slab = draw_slab(jax.random.fold_in(key_of[4], 71), 0)
    counts = with_ends(jax.random.randint(key_of[1], (TILES,), 0, TILE + 1), jax.random.fold_in(key_of[1], 1), 0, TILE).astype(jnp.int32)
    owner_keys = jax.random.split(jax.random.fold_in(key_of[2], 1), TILES // TPD)
    owner_turns = jax.random.permutation(jax.random.fold_in(key_of[2], 3), TILES // TPD)
    owner = jax.vmap(lambda own, number: deal_out(jax.random.fold_in(key_of[2], 2), own, number, TPD, N_SPACE, 1, CAP, 2))(owner_keys, owner_turns).reshape((TILES, 1))
    omega = normal_values(key_of[3], (TIME, K), TIME ** -0.5, 0.1875, ((0, 8),))
    return {"slab": slab, "counts": counts, "owner": owner, "omega": omega}


def reference(slab, counts, owner, omega):
    block = TIME // N_TM
    ocean = (jnp.arange(TILE)[None, :] < counts[:, None]).astype(jnp.float32)
    mean = lax.optimization_barrier(jnp.sum(slab, axis=2, dtype=jnp.float32)) / TIME
    anomalies = []
    total = jnp.zeros((TILES, TILE, K), jnp.float32)
    for index in range(N_TM):
        piece = lax.slice_in_dim(slab, index * block, (index + 1) * block, axis=2).astype(jnp.float32)
        anomaly = ((piece - mean[..., None]) * ocean[..., None]).astype(jnp.bfloat16)
        anomalies.append(anomaly)
        probes = lax.slice_in_dim(omega, index * block, (index + 1) * block, axis=0)
        term = jnp.einsum('ptc,ck->ptk', anomaly.astype(jnp.float32), probes.astype(jnp.float32))
        rounded = lax.optimization_barrier(term.astype(jnp.bfloat16))
        total = total + rounded.astype(jnp.float32)
    probe = total.astype(jnp.bfloat16)
    scale = 1.0 / jnp.sqrt(jnp.sum(counts.astype(jnp.float32)))
    blocks = []
    for index in range(N_TM):
        part = jnp.einsum('ptc,ptk->ck', anomalies[index].astype(jnp.float32), probe.astype(jnp.float32))
        blocks.append(part * scale)
    projected = jnp.concatenate(blocks, axis=0)
    targets = owner[:, 0].reshape(N_SPACE, TPD)
    onehot = (targets[..., None] == jnp.arange(N_SPACE)[None, None, :]).astype(jnp.int32)
    rank = lax.optimization_barrier(jnp.sum((jnp.cumsum(onehot, axis=1) - onehot) * onehot, axis=2))
    source = jnp.arange(N_SPACE, dtype=jnp.int32)[:, None]
    slots = (targets * (N_SPACE * CAP) + source * CAP + rank).reshape(TILES).astype(jnp.int32)
    probe_owned = jnp.zeros((SLOTS, TILE, K), jnp.bfloat16).at[slots].set(probe)
    return (probe_owned, projected)
```

```python
import functools

import jax
import jax.numpy as jnp
from jax import lax
from jax.experimental import pallas as pl
from jax.experimental.pallas import tpu as pltpu
from jax.sharding import PartitionSpec as P

MESH = pl.DeviceIdType.MESH
BF16 = jnp.bfloat16
F32 = jnp.float32
TIME = 1024
SIDE = 4
SPACES = SIDE * SIDE
TPD = 256
CAP = 24
CLASSES = CAP // 2
PER = -(-TPD // CAP)
PTS = 128
LANES = 128
PIECE = 16
STAGES = 7


def exchange(
    order, cnt, slot, omega, slab_hbm,
    rec, proj,
    slab, swp, swr, omr, rhs, wsend, wrecv, term, rs1, rs2, prb, cur, pack, ph1, ph2, back, vbuf, vrecv, half, ring,
    slab_sem, swap_s, swap_r, small_s, small_r, rs1_s, rs1_r, rs2_s, rs2_r, ag1_s, ag1_r, ag2_s, ag2_r,
    ph1_s, ph1_r, ph2_s, ph2_r, sis_s, sis_r, loc_s,
):
    space, tm = lax.axis_index("space"), lax.axis_index("tm")
    z, x = space // SIDE, space % SIDE
    y, c = tm // 2, tm % 2
    up, down, across = (y + 1) % SIDE, (y + 3) % SIDE, (y + 2) % SIDE
    a = jnp.where(c == 0, x, z)
    b = jnp.where(c == 0, z, x)

    sister = (space, y * 2 + (1 - c))

    def on_y(to):
        return (space, to * 2 + c)

    def on_ab(to_a, to_b):
        to_z = jnp.where(c == 0, to_b, to_a)
        to_x = jnp.where(c == 0, to_a, to_b)
        return (to_z * SIDE + to_x, tm)

    def remote(src, dst, send, recv, to):
        return pltpu.make_async_remote_copy(
            src_ref=src, dst_ref=dst, send_sem=send, recv_sem=recv, device_id=to, device_id_type=MESH
        )

    load = pltpu.make_async_copy(slab_hbm, slab, slab_sem)
    load.start()

    barrier = pltpu.get_barrier_semaphore()
    partners = [sister] + [on_y((y + d) % SIDE) for d in (1, 2, 3)]
    partners += [on_ab((a + d) % SIDE, b) for d in (1, 2, 3)] + [on_ab(a, (b + d) % SIDE) for d in (1, 2, 3)]
    for partner in partners:
        pl.semaphore_signal(barrier, inc=1, device_id=partner, device_id_type=MESH)
    pl.semaphore_wait(barrier, len(partners))

    om_copy = remote(omega, omr, small_s.at[0], small_r.at[0], sister)
    om_copy.start()

    def swap(j):
        return remote(swp.at[j], swr.at[j], swap_s.at[j], swap_r.at[j], sister)

    load.wait()

    @pl.loop(0, CLASSES)
    def _(j):
        @pl.loop(0, PER, unroll=True)
        def _(i):
            swp[j, i] = slab[order[CAP * i + 2 * j + 1 - c]]

        swap(j).start()

    cur[PER] = jnp.zeros((PTS, LANES), BF16)
    back[...] = jnp.zeros_like(back)

    om_copy.wait()
    rhs[:PTS, :LANES] = omega[...]
    rhs[PTS:, :LANES] = omr[...]
    rhs[:, LANES:] = jnp.ones((2 * PTS, LANES), BF16)
    both = omega[...].astype(F32) + omr[...].astype(F32)
    wsend[...] = jnp.broadcast_to(jnp.sum(both, axis=0, keepdims=True), wsend.shape)
    w_copies = [
        remote(wsend, wrecv.at[d - 1], small_s.at[d], small_r.at[d], on_y((y + d) % SIDE)) for d in (1, 2, 3)
    ]
    for copy in w_copies:
        copy.start()
    for copy in w_copies:
        copy.wait()
    wsend[...] = (wsend[...] + wrecv[0] + wrecv[1] + wrecv[2]) * (1.0 / TIME)

    def rs1_copies(j):
        return (
            remote(term.at[j, across, 0], rs1.at[j, 0], rs1_s.at[j, 0], rs1_r.at[j, 0], on_y(up)),
            remote(term.at[j, across, 1], rs1.at[j, 1], rs1_s.at[j, 1], rs1_r.at[j, 1], on_y(down)),
        )

    def rs2_copy(j, k):
        to = up if k < 2 else down
        return remote(term.at[j, to, k % 2], rs2.at[j, k], rs2_s.at[j, k], rs2_r.at[j, k], on_y(to))

    def ag1_copies(j):
        return (
            remote(prb.at[j, y], prb.at[j, y], ag1_s.at[j, 0], ag1_r.at[j, 0], on_y(up)),
            remote(prb.at[j, y], prb.at[j, y], ag1_s.at[j, 1], ag1_r.at[j, 1], on_y(down)),
        )

    def ag2_copies(j):
        return (
            remote(prb.at[j, down, 0], prb.at[j, down, 0], ag2_s.at[j, 0], ag2_r.at[j, 0], on_y(up)),
            remote(prb.at[j, up, 1], prb.at[j, up, 1], ag2_s.at[j, 1], ag2_r.at[j, 1], on_y(down)),
        )

    def ph1_copies(j):
        out = []
        for d in (1, 2, 3):
            to = (a + d) % SIDE
            out.append(
                remote(pack.at[j, to], ph1.at[j, :, a], ph1_s.at[j, d - 1], ph1_r.at[j, d - 1], on_ab(to, b))
            )
        return out

    def ph2_copies(j):
        out = []
        for d in (1, 2, 3):
            to = (b + d) % SIDE
            out.append(remote(ph1.at[j, to], ph2.at[j, b], ph2_s.at[j, d - 1], ph2_r.at[j, d - 1], on_ab(a, to)))
        return out

    def out_copies(j):
        return (
            remote(ph2.at[j], rec.at[c, j], sis_s.at[j], sis_r.at[j], sister),
            pltpu.make_async_copy(ph2.at[j], rec.at[c, j], loc_s.at[j]),
        )

    rows = lax.broadcasted_iota(jnp.int32, (PTS, LANES), 0)

    def terms(j):
        swap(j).wait_recv()
        mean_of = wsend[0:1, :]

        @pl.loop(0, PER, unroll=True)
        def _(i):
            at = CAP * i + 2 * j + c
            both_times = jnp.concatenate([slab[order[at]], swr[j, i]], axis=1)
            acc = jnp.dot(both_times, rhs[...], preferred_element_type=F32)
            value = acc[:, :LANES] - acc[:, LANES:] * mean_of
            value = jnp.where(rows < cnt[at], value, 0.0).astype(BF16)
            for q in range(SIDE):
                for h in range(2):
                    first = (2 * q + h) * PIECE
                    term[j, q, h, i] = value[first : first + PIECE]

        for copy in rs1_copies(j):
            copy.start()
        rs2_copy(j, 1).start()
        rs2_copy(j, 2).start()
        swap(j).wait_send()

    def add_across(j):
        for copy in rs1_copies(j):
            copy.wait_recv()
        term[j, up, 0] = (term[j, up, 0].astype(F32) + rs1[j, 0].astype(F32)).astype(BF16)
        rs2_copy(j, 0).start()
        term[j, down, 1] = (term[j, down, 1].astype(F32) + rs1[j, 1].astype(F32)).astype(BF16)
        rs2_copy(j, 3).start()
        for copy in rs1_copies(j):
            copy.wait_send()

    def finish_sum(j):
        for k in range(4):
            rs2_copy(j, k).wait_recv()
        for h in range(2):
            total = term[j, y, h].astype(F32) + rs2[j, h].astype(F32) + rs2[j, 2 + h].astype(F32)
            prb[j, y, h] = total.astype(BF16)
        for copy in ag1_copies(j):
            copy.start()
        for k in range(4):
            rs2_copy(j, k).wait_send()

    def forward(j):
        for copy in ag1_copies(j):
            copy.wait_recv()
        for copy in ag2_copies(j):
            copy.start()
        for copy in ag1_copies(j):
            copy.wait_send()

    def spread(j):
        for copy in ag2_copies(j):
            copy.wait_recv()

        for i in range(PER):
            for q in range(SIDE):
                for h in range(2):
                    first = (2 * q + h) * PIECE
                    cur[i, first : first + PIECE] = prb[j, q, h, i]

        for to_a in range(SIDE):
            for to_b in range(SIDE):
                pack[j, to_a, to_b] = cur[slot[SPACES * j + SIDE * to_a + to_b]]
        for copy in ph1_copies(j):
            copy.start()
        ph1[j, :, a] = pack[j, a]
        for copy in ag2_copies(j):
            copy.wait_send()

    def project(j):
        def one(i, total):
            both_times = jnp.concatenate([slab[order[CAP * i + 2 * j + c]], swr[j, i]], axis=1)
            return total + lax.dot_general(
                cur[i], both_times, (((0,), (0,)), ((), ())), preferred_element_type=F32
            )

        total = jnp.zeros((LANES, 2 * PTS), F32)
        for i in range(PER):
            total = one(i, total)
        back[...] += total

    def turn(j):
        for copy in ph1_copies(j):
            copy.wait_recv()
        for copy in ph2_copies(j):
            copy.start()
        ph2[j, b] = ph1[j, b]
        for copy in ph1_copies(j):
            copy.wait_send()

    def hand_over(j):
        for copy in ph2_copies(j):
            copy.wait_recv()
        for copy in out_copies(j):
            copy.start()
        for copy in ph2_copies(j):
            copy.wait_send()

    def leave(j):
        sis, loc = out_copies(j)
        sis.wait_send()
        loc.wait()

    def when(t, delay, stage):
        @pl.when((t >= delay) & (t < delay + CLASSES))
        def _():
            stage(t - delay)

    @pl.loop(0, CLASSES + 4)
    def _(t):
        when(t, 0, terms)
        when(t, 4, spread)
        when(t, 4, project)
        when(t, 1, add_across)
        when(t, 2, finish_sum)
        when(t, 3, forward)
        when(t, 5, turn)
        when(t, 6, hand_over)

    last = CLASSES - 1

    v = jnp.sum(back[...], axis=1, keepdims=True)
    vbuf[...] = jnp.broadcast_to(v, vbuf.shape)
    v_copies = [
        remote(vbuf, vrecv.at[d - 1], small_s.at[3 + d], small_r.at[3 + d], on_y((y + d) % SIDE)) for d in (1, 2, 3)
    ]
    for copy in v_copies:
        copy.start()
    hand_over(last - 1)
    turn(last)
    for copy in v_copies:
        copy.wait()
    mean = (vbuf[...] + vrecv[0] + vrecv[1] + vrecv[2]) * (1.0 / TIME)
    half[0] = back[:, :PTS] - mean
    half[1] = back[:, PTS:] - mean
    half_copy = remote(half.at[1], half.at[2], small_s.at[7], small_r.at[7], sister)
    half_copy.start()
    half_copy.wait()
    ring[0, 0] = half[0] + half[2]
    for axis in range(2):
        copies = []
        for d in (1, 2, 3):
            to = on_ab((a + d) % SIDE, b) if axis == 0 else on_ab(a, (b + d) % SIDE)
            copies.append(
                remote(ring.at[axis, 0], ring.at[axis, d], small_s.at[7 + 3 * axis + d], small_r.at[7 + 3 * axis + d], to)
            )
        for copy in copies:
            copy.start()
        if axis == 0:
            hand_over(last)
        for copy in copies:
            copy.wait()
        total = ring[axis, 0] + ring[axis, 1] + ring[axis, 2] + ring[axis, 3]
        if axis == 0:
            ring[1, 0] = total
        else:
            proj[...] = total

    for j in range(CLASSES):
        leave(j)
    for j in range(CLASSES):
        out_copies(j)[0].wait_recv()


def place(table, rec, proj, scale, out, proj_out, sem):
    @pl.loop(0, SPACES * CAP)
    def _(n):
        pltpu.make_async_copy(rec.at[table[n]], out.at[n], sem).start()

    proj_out[...] = proj[...].T * scale[0, 0]
    pltpu.make_async_copy(rec, out, sem).wait()


def local(slab, counts, owner, omega):
    space, tm = lax.axis_index("space"), lax.axis_index("tm")
    c = tm % 2
    names = owner.reshape(SPACES, TPD)
    first = jnp.sum(
        (names[:, None, :] < jnp.arange(SPACES + 1, dtype=jnp.int32)[None, :, None]).astype(jnp.int32), axis=2
    )
    mine = lax.dynamic_index_in_dim(names, space, 0, keepdims=False)
    tiles = jnp.arange(TPD, dtype=jnp.int32)
    key = mine * TPD + tiles
    spot = jnp.sum((key[None, :] < key[:, None]).astype(jnp.int32), axis=1)
    places = jnp.arange(PER * CAP, dtype=jnp.int32)
    hit = spot[None, :] == places[:, None]
    order = jnp.sum(jnp.where(hit, tiles[None, :], 0), axis=1)
    points = lax.dynamic_slice_in_dim(counts, space * TPD, TPD)
    cnt = jnp.sum(jnp.where(hit, points[None, :], 0), axis=1)

    my_first = lax.dynamic_index_in_dim(first, space, 0, keepdims=False)
    begin, end = my_first[:-1], my_first[1:]
    cls = 2 * jnp.arange(CLASSES, dtype=jnp.int32)[:, None] + c
    spot_of = begin[None, :] + (cls - begin[None, :]) % CAP
    slot = jnp.where(spot_of < end[None, :], spot_of // CAP, PER).reshape(CLASSES, SIDE, SIDE)
    slot = jnp.where(c == 0, slot.swapaxes(1, 2), slot).reshape(-1)

    starts = lax.dynamic_index_in_dim(first, space, 1, keepdims=False)
    where = (starts[:, None] + jnp.arange(CAP, dtype=jnp.int32)[None, :]) % CAP
    source = jnp.arange(SPACES, dtype=jnp.int32)[:, None]
    turned = (source % SIDE) * SIDE + source // SIDE
    table = ((where % 2) * CLASSES + where // 2) * SPACES + jnp.where(where % 2 == 0, source, turned)

    scale = 1.0 / jnp.sqrt(jnp.sum(counts.astype(F32)))

    smem, vmem, hbm = (pl.BlockSpec(memory_space=m) for m in (pltpu.SMEM, pltpu.VMEM, pl.ANY))
    dma = pltpu.SemaphoreType.DMA
    piece = (PER, PIECE, LANES)
    tile = (PTS, LANES)
    rec, proj = pl.pallas_call(
        exchange,
        out_shape=(
            jax.ShapeDtypeStruct((2, CLASSES, SIDE, SIDE) + tile, BF16),
            jax.ShapeDtypeStruct(tile, F32),
        ),
        in_specs=[smem, smem, smem, vmem, hbm],
        out_specs=(hbm, vmem),
        scratch_shapes=[
            pltpu.VMEM((TPD,) + tile, BF16),
            pltpu.VMEM((CLASSES, PER) + tile, BF16),
            pltpu.VMEM((CLASSES, PER) + tile, BF16),
            pltpu.VMEM(tile, BF16),
            pltpu.VMEM((2 * PTS, 2 * LANES), BF16),
            pltpu.VMEM((8, LANES), F32),
            pltpu.VMEM((3, 8, LANES), F32),
            pltpu.VMEM((CLASSES, SIDE, 2) + piece, BF16),
            pltpu.VMEM((CLASSES, 2) + piece, BF16),
            pltpu.VMEM((CLASSES, 4) + piece, BF16),
            pltpu.VMEM((CLASSES, SIDE, 2) + piece, BF16),
            pltpu.VMEM((PER + 1,) + tile, BF16),
            pltpu.VMEM((CLASSES, SIDE, SIDE) + tile, BF16),
            pltpu.VMEM((CLASSES, SIDE, SIDE) + tile, BF16),
            pltpu.VMEM((CLASSES, SIDE, SIDE) + tile, BF16),
            pltpu.VMEM((LANES, 2 * PTS), F32),
            pltpu.VMEM((LANES, LANES), F32),
            pltpu.VMEM((3, LANES, LANES), F32),
            pltpu.VMEM((3, LANES, PTS), F32),
            pltpu.VMEM((2, SIDE, LANES, PTS), F32),
            dma,
            dma((CLASSES,)), dma((CLASSES,)),
            dma((14,)), dma((14,)),
            dma((CLASSES, 2)), dma((CLASSES, 2)),
            dma((CLASSES, 4)), dma((CLASSES, 4)),
            dma((CLASSES, 2)), dma((CLASSES, 2)),
            dma((CLASSES, 2)), dma((CLASSES, 2)),
            dma((CLASSES, 3)), dma((CLASSES, 3)),
            dma((CLASSES, 3)), dma((CLASSES, 3)),
            dma((CLASSES,)), dma((CLASSES,)), dma((CLASSES,)),
        ],
        compiler_params=pltpu.CompilerParams(
            collective_id=0, has_side_effects=True, vmem_limit_bytes=60 << 20
        ),
        name="exchange",
    )(order, cnt, slot, omega, slab)
    probe_owned, projected = pl.pallas_call(
        place,
        out_shape=(
            jax.ShapeDtypeStruct((SPACES * CAP,) + tile, BF16),
            jax.ShapeDtypeStruct(tile, F32),
        ),
        in_specs=[smem, hbm, vmem, smem],
        out_specs=(hbm, vmem),
        scratch_shapes=[dma],
        compiler_params=pltpu.CompilerParams(vmem_limit_bytes=16 << 20),
        name="place",
    )(table.reshape(-1), rec.reshape((SPACES * CAP,) + tile), proj, scale.reshape(1, 1))
    return probe_owned, projected


def solution(mesh):
    return jax.shard_map(
        local,
        mesh=mesh,
        in_specs=(P("space", None, "tm"), P(), P(), P("tm", None)),
        out_specs=(P("space", None, None), P("tm", None)),
        check_vma=False,
    )
```

```python
import functools

import jax
import jax.numpy as jnp
from jax import lax
from jax.experimental import pallas as pl
from jax.experimental.pallas import tpu as pltpu
from jax.sharding import PartitionSpec as P

MESH = pl.DeviceIdType.MESH
BF16 = jnp.bfloat16
F32 = jnp.float32
TIME = 1024
SIDE = 4
SPACES = SIDE * SIDE
TPD = 256
CAP = 24
CLASSES = CAP // 2
PER = -(-TPD // CAP)
PTS = 128
LANES = 128
PIECE = 16
DELAYS = (0, 1, 2, 3, 4, 6, 8)


def exchange(
    order, cnt, slot, omega, slab_hbm,
    rec, proj,
    slab, swp, swr, omr, rhs, wsend, wrecv, term, rs1, rs2, prb, cur, pack, ph1, back, vbuf, vrecv, half, ring,
    slab_sem, swap_s, swap_r, small_s, small_r, rs1_s, rs1_r, rs2_s, rs2_r, ag1_s, ag1_r, ag2_s, ag2_r,
    ph1_s, ph1_r, ph2_s, ph2_r, sis_s, sis_r,
):
    space, tm = lax.axis_index("space"), lax.axis_index("tm")
    z, x = space // SIDE, space % SIDE
    y, c = tm // 2, tm % 2
    up, down, across = (y + 1) % SIDE, (y + 3) % SIDE, (y + 2) % SIDE
    a = jnp.where(c == 0, x, z)
    b = jnp.where(c == 0, z, x)

    sister = (space, y * 2 + (1 - c))

    def on_y(to):
        return (space, to * 2 + c)

    def on_ab(to_a, to_b):
        to_z = jnp.where(c == 0, to_b, to_a)
        to_x = jnp.where(c == 0, to_a, to_b)
        return (to_z * SIDE + to_x, tm)

    def remote(src, dst, send, recv, to):
        return pltpu.make_async_remote_copy(
            src_ref=src, dst_ref=dst, send_sem=send, recv_sem=recv, device_id=to, device_id_type=MESH
        )

    load = pltpu.make_async_copy(slab_hbm, slab, slab_sem)
    load.start()

    barrier = pltpu.get_barrier_semaphore()
    partners = [sister] + [on_y((y + d) % SIDE) for d in (1, 2, 3)]
    partners += [on_ab((a + d) % SIDE, b) for d in (1, 2, 3)] + [on_ab(a, (b + d) % SIDE) for d in (1, 2, 3)]
    for partner in partners:
        pl.semaphore_signal(barrier, inc=1, device_id=partner, device_id_type=MESH)
    pl.semaphore_wait(barrier, len(partners))

    om_copy = remote(omega, omr, small_s.at[0], small_r.at[0], sister)
    om_copy.start()

    def swap(j):
        return remote(swp.at[j], swr.at[j], swap_s.at[j], swap_r.at[j], sister)

    load.wait()

    @pl.loop(0, CLASSES)
    def _(j):
        @pl.loop(0, PER, unroll=True)
        def _(i):
            swp[j, i] = slab[order[CAP * i + 2 * j + 1 - c]]

        swap(j).start()

    cur[PER] = jnp.zeros((PTS, LANES), BF16)
    back[...] = jnp.zeros_like(back)

    om_copy.wait()
    rhs[:PTS, :LANES] = omega[...]
    rhs[PTS:, :LANES] = omr[...]
    rhs[:, LANES:] = jnp.ones((2 * PTS, LANES), BF16)
    both = omega[...].astype(F32) + omr[...].astype(F32)
    wsend[...] = jnp.broadcast_to(jnp.sum(both, axis=0, keepdims=True), wsend.shape)
    w_copies = [
        remote(wsend, wrecv.at[d - 1], small_s.at[d], small_r.at[d], on_y((y + d) % SIDE)) for d in (1, 2, 3)
    ]
    for copy in w_copies:
        copy.start()
    for copy in w_copies:
        copy.wait()
    wsend[...] = (wsend[...] + wrecv[0] + wrecv[1] + wrecv[2]) * (1.0 / TIME)

    def rs1_copies(j):
        return (
            remote(term.at[j, across, 0], rs1.at[j, 0], rs1_s.at[j, 0], rs1_r.at[j, 0], on_y(up)),
            remote(term.at[j, across, 1], rs1.at[j, 1], rs1_s.at[j, 1], rs1_r.at[j, 1], on_y(down)),
        )

    def rs2_copy(j, k):
        to = up if k < 2 else down
        return remote(term.at[j, to, k % 2], rs2.at[j, k], rs2_s.at[j, k], rs2_r.at[j, k], on_y(to))

    def ag1_copies(j):
        return (
            remote(prb.at[j, y], prb.at[j, y], ag1_s.at[j, 0], ag1_r.at[j, 0], on_y(up)),
            remote(prb.at[j, y], prb.at[j, y], ag1_s.at[j, 1], ag1_r.at[j, 1], on_y(down)),
        )

    def ag2_copies(j):
        return (
            remote(prb.at[j, down, 0], prb.at[j, down, 0], ag2_s.at[j, 0], ag2_r.at[j, 0], on_y(up)),
            remote(prb.at[j, up, 1], prb.at[j, up, 1], ag2_s.at[j, 1], ag2_r.at[j, 1], on_y(down)),
        )

    def ph1_copies(j):
        out = []
        for d in (1, 2, 3):
            to = (a + d) % SIDE
            out.append(
                remote(pack.at[j, to], ph1.at[j, :, a], ph1_s.at[j, d - 1], ph1_r.at[j, d - 1], on_ab(to, b))
            )
        return out

    def ph2_copies(j):
        out = []
        for d in (1, 2, 3):
            to = (b + d) % SIDE
            out.append(remote(ph1.at[j, to], rec.at[c, j, b], ph2_s.at[j, d - 1], ph2_r.at[j, d - 1], on_ab(a, to)))
        return out

    def out_copy(j):
        return remote(rec.at[c, j], rec.at[c, j], sis_s.at[j], sis_r.at[j], sister)

    rows = lax.broadcasted_iota(jnp.int32, (PTS, LANES), 0)

    def terms(j):
        swap(j).wait_recv()
        mean_of = wsend[0:1, :]

        @pl.loop(0, PER, unroll=True)
        def _(i):
            at = CAP * i + 2 * j + c
            both_times = jnp.concatenate([slab[order[at]], swr[j, i]], axis=1)
            acc = jnp.dot(both_times, rhs[...], preferred_element_type=F32)
            value = acc[:, :LANES] - acc[:, LANES:] * mean_of
            value = jnp.where(rows < cnt[at], value, 0.0).astype(BF16)
            for q in range(SIDE):
                for h in range(2):
                    first = (2 * q + h) * PIECE
                    term[j, q, h, i] = value[first : first + PIECE]

        for copy in rs1_copies(j):
            copy.start()
        rs2_copy(j, 1).start()
        rs2_copy(j, 2).start()
        swap(j).wait_send()

    def add_across(j):
        for copy in rs1_copies(j):
            copy.wait_recv()
        term[j, up, 0] = (term[j, up, 0].astype(F32) + rs1[j, 0].astype(F32)).astype(BF16)
        rs2_copy(j, 0).start()
        term[j, down, 1] = (term[j, down, 1].astype(F32) + rs1[j, 1].astype(F32)).astype(BF16)
        rs2_copy(j, 3).start()
        for copy in rs1_copies(j):
            copy.wait_send()

    def finish_sum(j):
        for k in range(4):
            rs2_copy(j, k).wait_recv()
        for h in range(2):
            total = term[j, y, h].astype(F32) + rs2[j, h].astype(F32) + rs2[j, 2 + h].astype(F32)
            prb[j, y, h] = total.astype(BF16)
        for copy in ag1_copies(j):
            copy.start()
        for k in range(4):
            rs2_copy(j, k).wait_send()

    def forward(j):
        for copy in ag1_copies(j):
            copy.wait_recv()
        for copy in ag2_copies(j):
            copy.start()
        for copy in ag1_copies(j):
            copy.wait_send()

    def spread(j):
        for copy in ag2_copies(j):
            copy.wait_recv()

        for i in range(PER):
            for q in range(SIDE):
                for h in range(2):
                    first = (2 * q + h) * PIECE
                    cur[i, first : first + PIECE] = prb[j, q, h, i]

        for to_a in range(SIDE):
            for to_b in range(SIDE):
                pack[j, to_a, to_b] = cur[slot[SPACES * j + SIDE * to_a + to_b]]
        for copy in ph1_copies(j):
            copy.start()
        ph1[j, :, a] = pack[j, a]
        for copy in ag2_copies(j):
            copy.wait_send()

    def project(j):
        def one(i, total):
            both_times = jnp.concatenate([slab[order[CAP * i + 2 * j + c]], swr[j, i]], axis=1)
            return total + lax.dot_general(
                cur[i], both_times, (((0,), (0,)), ((), ())), preferred_element_type=F32
            )

        total = jnp.zeros((LANES, 2 * PTS), F32)
        for i in range(PER):
            total = one(i, total)
        back[...] += total

    def turn(j):
        for copy in ph1_copies(j):
            copy.wait_recv()
        for copy in ph2_copies(j):
            copy.start()
        rec[c, j, b] = ph1[j, b]
        for copy in ph1_copies(j):
            copy.wait_send()

    def hand_over(j):
        for copy in ph2_copies(j):
            copy.wait_recv()
        out_copy(j).start()
        for copy in ph2_copies(j):
            copy.wait_send()

    def when(t, delay, stage):
        @pl.when((t >= delay) & (t < delay + CLASSES))
        def _():
            stage(t - delay)

    def v_copies():
        return [
            remote(vbuf, vrecv.at[d - 1], small_s.at[3 + d], small_r.at[3 + d], on_y((y + d) % SIDE))
            for d in (1, 2, 3)
        ]

    def half_copy():
        return remote(half.at[1], half.at[2], small_s.at[7], small_r.at[7], sister)

    def ring_copies(axis):
        copies = []
        for d in (1, 2, 3):
            to = on_ab((a + d) % SIDE, b) if axis == 0 else on_ab(a, (b + d) % SIDE)
            k = 7 + 3 * axis + d
            copies.append(remote(ring.at[axis, 0], ring.at[axis, d], small_s.at[k], small_r.at[k], to))
        return copies

    def back_sum():
        v = jnp.sum(back[...], axis=1, keepdims=True)
        vbuf[...] = jnp.broadcast_to(v, vbuf.shape)
        for copy in v_copies():
            copy.start()

    def back_centre():
        for copy in v_copies():
            copy.wait()
        mean = (vbuf[...] + vrecv[0] + vrecv[1] + vrecv[2]) * (1.0 / TIME)
        half[0] = back[:, :PTS] - mean
        half[1] = back[:, PTS:] - mean
        half_copy().start()

    def back_cores():
        half_copy().wait()
        ring[0, 0] = half[0] + half[2]
        for copy in ring_copies(0):
            copy.start()

    def back_first():
        for copy in ring_copies(0):
            copy.wait()
        ring[1, 0] = ring[0, 0] + ring[0, 1] + ring[0, 2] + ring[0, 3]
        for copy in ring_copies(1):
            copy.start()

    def back_second():
        for copy in ring_copies(1):
            copy.wait()
        proj[...] = ring[1, 0] + ring[1, 1] + ring[1, 2] + ring[1, 3]

    def once(t, at, stage):
        @pl.when(t == at)
        def _():
            stage()

    ended = CLASSES - 1 + DELAYS[4]

    @pl.loop(0, max(CLASSES + DELAYS[6], ended + 5))
    def _(t):
        when(t, DELAYS[0], terms)
        when(t, DELAYS[4], spread)
        when(t, DELAYS[1], add_across)
        when(t, DELAYS[2], finish_sum)
        when(t, DELAYS[3], forward)
        when(t, DELAYS[5], turn)
        when(t, DELAYS[6], hand_over)
        when(t, DELAYS[4], project)
        once(t, ended, back_sum)
        once(t, ended + 1, back_centre)
        once(t, ended + 1, back_cores)
        once(t, ended + 2, back_first)
        once(t, ended + 3, back_second)

    for j in range(CLASSES):
        out_copy(j).wait()


def place(table, rec, proj, scale, out, proj_out, sem):
    @pl.loop(0, SPACES * CAP)
    def _(n):
        pltpu.make_async_copy(rec.at[table[n]], out.at[n], sem).start()

    proj_out[...] = proj[...].T * scale[0, 0]
    pltpu.make_async_copy(rec, out, sem).wait()


def local(slab, counts, owner, omega):
    space, tm = lax.axis_index("space"), lax.axis_index("tm")
    c = tm % 2
    names = owner.reshape(SPACES, TPD)
    first = jnp.sum(
        (names[:, None, :] < jnp.arange(SPACES + 1, dtype=jnp.int32)[None, :, None]).astype(jnp.int32), axis=2
    )
    mine = lax.dynamic_index_in_dim(names, space, 0, keepdims=False)
    tiles = jnp.arange(TPD, dtype=jnp.int32)
    key = mine * TPD + tiles
    spot = jnp.sum((key[None, :] < key[:, None]).astype(jnp.int32), axis=1)
    places = jnp.arange(PER * CAP, dtype=jnp.int32)
    hit = spot[None, :] == places[:, None]
    order = jnp.sum(jnp.where(hit, tiles[None, :], 0), axis=1)
    points = lax.dynamic_slice_in_dim(counts, space * TPD, TPD)
    cnt = jnp.sum(jnp.where(hit, points[None, :], 0), axis=1)

    my_first = lax.dynamic_index_in_dim(first, space, 0, keepdims=False)
    begin, end = my_first[:-1], my_first[1:]
    cls = 2 * jnp.arange(CLASSES, dtype=jnp.int32)[:, None] + c
    spot_of = begin[None, :] + (cls - begin[None, :]) % CAP
    slot = jnp.where(spot_of < end[None, :], spot_of // CAP, PER).reshape(CLASSES, SIDE, SIDE)
    slot = jnp.where(c == 0, slot.swapaxes(1, 2), slot).reshape(-1)

    starts = lax.dynamic_index_in_dim(first, space, 1, keepdims=False)
    where = (starts[:, None] + jnp.arange(CAP, dtype=jnp.int32)[None, :]) % CAP
    source = jnp.arange(SPACES, dtype=jnp.int32)[:, None]
    turned = (source % SIDE) * SIDE + source // SIDE
    table = ((where % 2) * CLASSES + where // 2) * SPACES + jnp.where(where % 2 == 0, source, turned)

    scale = 1.0 / jnp.sqrt(jnp.sum(counts.astype(F32)))

    smem, vmem, hbm = (pl.BlockSpec(memory_space=m) for m in (pltpu.SMEM, pltpu.VMEM, pl.ANY))
    dma = pltpu.SemaphoreType.DMA
    piece = (PER, PIECE, LANES)
    tile = (PTS, LANES)
    rec, proj = pl.pallas_call(
        exchange,
        out_shape=(
            pltpu.VMEM((2, CLASSES, SIDE, SIDE) + tile, BF16),
            jax.ShapeDtypeStruct(tile, F32),
        ),
        in_specs=[smem, smem, smem, vmem, hbm],
        out_specs=(vmem, vmem),
        scratch_shapes=[
            pltpu.VMEM((TPD,) + tile, BF16),
            pltpu.VMEM((CLASSES, PER) + tile, BF16),
            pltpu.VMEM((CLASSES, PER) + tile, BF16),
            pltpu.VMEM(tile, BF16),
            pltpu.VMEM((2 * PTS, 2 * LANES), BF16),
            pltpu.VMEM((8, LANES), F32),
            pltpu.VMEM((3, 8, LANES), F32),
            pltpu.VMEM((CLASSES, SIDE, 2) + piece, BF16),
            pltpu.VMEM((CLASSES, 2) + piece, BF16),
            pltpu.VMEM((CLASSES, 4) + piece, BF16),
            pltpu.VMEM((CLASSES, SIDE, 2) + piece, BF16),
            pltpu.VMEM((PER + 1,) + tile, BF16),
            pltpu.VMEM((CLASSES, SIDE, SIDE) + tile, BF16),
            pltpu.VMEM((CLASSES, SIDE, SIDE) + tile, BF16),
            pltpu.VMEM((LANES, 2 * PTS), F32),
            pltpu.VMEM((LANES, LANES), F32),
            pltpu.VMEM((3, LANES, LANES), F32),
            pltpu.VMEM((3, LANES, PTS), F32),
            pltpu.VMEM((2, SIDE, LANES, PTS), F32),
            dma,
            dma((CLASSES,)), dma((CLASSES,)),
            dma((14,)), dma((14,)),
            dma((CLASSES, 2)), dma((CLASSES, 2)),
            dma((CLASSES, 4)), dma((CLASSES, 4)),
            dma((CLASSES, 2)), dma((CLASSES, 2)),
            dma((CLASSES, 2)), dma((CLASSES, 2)),
            dma((CLASSES, 3)), dma((CLASSES, 3)),
            dma((CLASSES, 3)), dma((CLASSES, 3)),
            dma((CLASSES,)), dma((CLASSES,)),
        ],
        compiler_params=pltpu.CompilerParams(
            collective_id=0, has_side_effects=True, vmem_limit_bytes=46 << 20
        ),
        name="exchange",
    )(order, cnt, slot, omega, slab)
    probe_owned, projected = pl.pallas_call(
        place,
        out_shape=(
            jax.ShapeDtypeStruct((SPACES * CAP,) + tile, BF16),
            jax.ShapeDtypeStruct(tile, F32),
        ),
        in_specs=[smem, hbm, vmem, smem],
        out_specs=(hbm, vmem),
        scratch_shapes=[dma],
        compiler_params=pltpu.CompilerParams(vmem_limit_bytes=16 << 20),
        name="place",
    )(table.reshape(-1), rec.reshape((SPACES * CAP,) + tile), proj, scale.reshape(1, 1))
    return probe_owned, projected


def solution(mesh):
    return jax.shard_map(
        local,
        mesh=mesh,
        in_specs=(P("space", None, "tm"), P(), P(), P("tm", None)),
        out_specs=(P("space", None, None), P("tm", None)),
        check_vma=False,
    )
```

```python
import functools

import jax
import jax.numpy as jnp
from jax import lax
from jax.experimental import pallas as pl
from jax.experimental.pallas import tpu as pltpu
from jax.sharding import PartitionSpec as P

MESH = pl.DeviceIdType.MESH
BF16 = jnp.bfloat16
F32 = jnp.float32
TIME = 1024
SIDE = 4
SPACES = SIDE * SIDE
TPD = 256
CAP = 24
CLASSES = CAP // 2
PER = -(-TPD // CAP)
PTS = 128
LANES = 128
PIECE = 16
DELAYS = (0, 1, 2, 3, 4, 6, 8)


def exchange(
    names, counts, omega, slab_hbm,
    rec, proj, info,
    tab_v, tab, slab, swp, swr, omr, rhs, wsend, wrecv, term, rs1, rs2, prb, cur, pack, ph1, back, vbuf, vrecv, half, ring,
    tab_sem, slab_sem, swap_s, swap_r, small_s, small_r, rs1_s, rs1_r, rs2_s, rs2_r, ag1_s, ag1_r, ag2_s, ag2_r,
    ph1_s, ph1_r, ph2_s, ph2_r, sis_s, sis_r,
):
    space, tm = lax.axis_index("space"), lax.axis_index("tm")
    z, x = space // SIDE, space % SIDE
    y, c = tm // 2, tm % 2
    up, down, across = (y + 1) % SIDE, (y + 3) % SIDE, (y + 2) % SIDE
    a = jnp.where(c == 0, x, z)
    b = jnp.where(c == 0, z, x)

    sister = (space, y * 2 + (1 - c))

    def on_y(to):
        return (space, to * 2 + c)

    def on_ab(to_a, to_b):
        to_z = jnp.where(c == 0, to_b, to_a)
        to_x = jnp.where(c == 0, to_a, to_b)
        return (to_z * SIDE + to_x, tm)

    def remote(src, dst, send, recv, to):
        return pltpu.make_async_remote_copy(
            src_ref=src, dst_ref=dst, send_sem=send, recv_sem=recv, device_id=to, device_id_type=MESH
        )

    load = pltpu.make_async_copy(slab_hbm, slab, slab_sem)
    load.start()

    barrier = pltpu.get_barrier_semaphore()
    partners = [sister] + [on_y((y + d) % SIDE) for d in (1, 2, 3)]
    partners += [on_ab((a + d) % SIDE, b) for d in (1, 2, 3)] + [on_ab(a, (b + d) % SIDE) for d in (1, 2, 3)]
    for partner in partners:
        pl.semaphore_signal(barrier, inc=1, device_id=partner, device_id_type=MESH)

    lane = lax.broadcasted_iota(jnp.int32, (PTS, LANES), 1)
    row = lax.broadcasted_iota(jnp.int32, (PTS, LANES), 0)
    own = [jnp.broadcast_to(names[pl.ds(2 * space + h, 1), :], (PTS, LANES)) for h in range(2)]
    points = [jnp.broadcast_to(counts[pl.ds(2 * space + h, 1), :], (PTS, LANES)) for h in range(2)]
    keys = [own[h] * TPD + (lane + LANES * h) for h in range(2)]
    order_of, begins = [0] * 3, 0
    for h in range(2):
        key = keys[h].T
        before = sum(jnp.where(keys[g] < key, 1, 0) for g in range(2))
        spot = jnp.sum(before, axis=1, keepdims=True)
        code = (row + PTS * h) * 256 + points[h].T
        for g in range(3):
            hit = jnp.where(spot == lane + LANES * g, code, 0)
            order_of[g] = order_of[g] + jnp.sum(hit, axis=0, keepdims=True)
        begins = begins + jnp.sum(jnp.where(own[h].T < lane, 1, 0), axis=0, keepdims=True)
    for g in range(3):
        tab_v[:, LANES * g : LANES * (g + 1)] = jnp.broadcast_to(order_of[g], (8, LANES))
    tab_v[:, 3 * LANES :] = jnp.broadcast_to(begins, (8, LANES))
    tab_copy = pltpu.make_async_copy(tab_v, tab, tab_sem)
    tab_copy.start()
    lower = jnp.where(names[...] < space, 1, 0)
    info[...] = jnp.broadcast_to(jnp.sum(lower, axis=1, keepdims=True), info.shape)

    def tile_at(place):
        return jnp.clip(lax.div(tab[0, place], 256), 0, TPD - 1)

    def count_at(place):
        return lax.rem(tab[0, place], 256)

    def tile_for(j, owner):
        begin, end = tab[0, 3 * LANES + owner], tab[0, 3 * LANES + 1 + owner]
        place = begin + lax.rem(2 * j + c + PER * CAP - begin, CAP)
        return jnp.where(place < end, jnp.clip(lax.div(place, CAP), 0, PER), PER)

    pl.semaphore_wait(barrier, len(partners))

    om_copy = remote(omega, omr, small_s.at[0], small_r.at[0], sister)
    om_copy.start()
    om_copy.wait()
    both = omega[...].astype(F32) + omr[...].astype(F32)
    wsend[...] = jnp.broadcast_to(jnp.sum(both, axis=0, keepdims=True), wsend.shape)
    w_copies = [
        remote(wsend, wrecv.at[d - 1], small_s.at[d], small_r.at[d], on_y((y + d) % SIDE)) for d in (1, 2, 3)
    ]
    for copy in w_copies:
        copy.start()
    rhs[:PTS, :LANES] = omega[...]
    rhs[PTS:, :LANES] = omr[...]
    rhs[:, LANES:] = jnp.ones((2 * PTS, LANES), BF16)
    cur[PER] = jnp.zeros((PTS, LANES), BF16)
    back[...] = jnp.zeros_like(back)

    def swap(j):
        return remote(swp.at[j], swr.at[j], swap_s.at[j], swap_r.at[j], sister)

    tab_copy.wait()
    load.wait()

    @pl.loop(0, CLASSES)
    def _(j):
        @pl.loop(0, PER, unroll=True)
        def _(i):
            swp[j, i] = slab[tile_at(CAP * i + 2 * j + 1 - c)]

        swap(j).start()

    for copy in w_copies:
        copy.wait()
    wsend[...] = (wsend[...] + wrecv[0] + wrecv[1] + wrecv[2]) * (1.0 / TIME)

    def rs1_copies(j):
        return (
            remote(term.at[j, across, 0], rs1.at[j, 0], rs1_s.at[j, 0], rs1_r.at[j, 0], on_y(up)),
            remote(term.at[j, across, 1], rs1.at[j, 1], rs1_s.at[j, 1], rs1_r.at[j, 1], on_y(down)),
        )

    def rs2_copy(j, k):
        to = up if k < 2 else down
        return remote(term.at[j, to, k % 2], rs2.at[j, k], rs2_s.at[j, k], rs2_r.at[j, k], on_y(to))

    def ag1_copies(j):
        return (
            remote(prb.at[j, y], prb.at[j, y], ag1_s.at[j, 0], ag1_r.at[j, 0], on_y(up)),
            remote(prb.at[j, y], prb.at[j, y], ag1_s.at[j, 1], ag1_r.at[j, 1], on_y(down)),
        )

    def ag2_copies(j):
        return (
            remote(prb.at[j, down, 0], prb.at[j, down, 0], ag2_s.at[j, 0], ag2_r.at[j, 0], on_y(up)),
            remote(prb.at[j, up, 1], prb.at[j, up, 1], ag2_s.at[j, 1], ag2_r.at[j, 1], on_y(down)),
        )

    def ph1_copies(j):
        out = []
        for d in (1, 2, 3):
            to = (a + d) % SIDE
            out.append(
                remote(pack.at[j, to], ph1.at[j, :, a], ph1_s.at[j, d - 1], ph1_r.at[j, d - 1], on_ab(to, b))
            )
        return out

    def ph2_copies(j):
        out = []
        for d in (1, 2, 3):
            to = (b + d) % SIDE
            out.append(remote(ph1.at[j, to], rec.at[c, j, b], ph2_s.at[j, d - 1], ph2_r.at[j, d - 1], on_ab(a, to)))
        return out

    def out_copy(j):
        return remote(rec.at[c, j], rec.at[c, j], sis_s.at[j], sis_r.at[j], sister)

    rows = lax.broadcasted_iota(jnp.int32, (PTS, LANES), 0)

    def terms(j):
        swap(j).wait_recv()
        mean_of = wsend[0:1, :]

        @pl.loop(0, PER, unroll=True)
        def _(i):
            at = CAP * i + 2 * j + c
            both_times = jnp.concatenate([slab[tile_at(at)], swr[j, i]], axis=1)
            acc = jnp.dot(both_times, rhs[...], preferred_element_type=F32)
            value = acc[:, :LANES] - acc[:, LANES:] * mean_of
            value = jnp.where(rows < count_at(at), value, 0.0).astype(BF16)
            for q in range(SIDE):
                for h in range(2):
                    first = (2 * q + h) * PIECE
                    term[j, q, h, i] = value[first : first + PIECE]

        for copy in rs1_copies(j):
            copy.start()
        rs2_copy(j, 1).start()
        rs2_copy(j, 2).start()
        swap(j).wait_send()

    def add_across(j):
        for copy in rs1_copies(j):
            copy.wait_recv()
        term[j, up, 0] = (term[j, up, 0].astype(F32) + rs1[j, 0].astype(F32)).astype(BF16)
        rs2_copy(j, 0).start()
        term[j, down, 1] = (term[j, down, 1].astype(F32) + rs1[j, 1].astype(F32)).astype(BF16)
        rs2_copy(j, 3).start()
        for copy in rs1_copies(j):
            copy.wait_send()

    def finish_sum(j):
        for k in range(4):
            rs2_copy(j, k).wait_recv()
        for h in range(2):
            total = term[j, y, h].astype(F32) + rs2[j, h].astype(F32) + rs2[j, 2 + h].astype(F32)
            prb[j, y, h] = total.astype(BF16)
        for copy in ag1_copies(j):
            copy.start()
        for k in range(4):
            rs2_copy(j, k).wait_send()

    def forward(j):
        for copy in ag1_copies(j):
            copy.wait_recv()
        for copy in ag2_copies(j):
            copy.start()
        for copy in ag1_copies(j):
            copy.wait_send()

    def spread(j):
        for copy in ag2_copies(j):
            copy.wait_recv()

        for i in range(PER):
            for q in range(SIDE):
                for h in range(2):
                    first = (2 * q + h) * PIECE
                    cur[i, first : first + PIECE] = prb[j, q, h, i]

        for to_a in range(SIDE):
            for to_b in range(SIDE):
                owner = jnp.where(c == 0, SIDE * to_b + to_a, SIDE * to_a + to_b)
                pack[j, to_a, to_b] = cur[tile_for(j, owner)]
        for copy in ph1_copies(j):
            copy.start()
        ph1[j, :, a] = pack[j, a]
        for copy in ag2_copies(j):
            copy.wait_send()

    def project(j):
        def one(i, total):
            both_times = jnp.concatenate([slab[tile_at(CAP * i + 2 * j + c)], swr[j, i]], axis=1)
            return total + lax.dot_general(
                cur[i], both_times, (((0,), (0,)), ((), ())), preferred_element_type=F32
            )

        total = jnp.zeros((LANES, 2 * PTS), F32)
        for i in range(PER):
            total = one(i, total)
        back[...] += total

    def turn(j):
        for copy in ph1_copies(j):
            copy.wait_recv()
        for copy in ph2_copies(j):
            copy.start()
        rec[c, j, b] = ph1[j, b]
        for copy in ph1_copies(j):
            copy.wait_send()

    def hand_over(j):
        for copy in ph2_copies(j):
            copy.wait_recv()
        out_copy(j).start()
        for copy in ph2_copies(j):
            copy.wait_send()

    def when(t, delay, stage):
        @pl.when((t >= delay) & (t < delay + CLASSES))
        def _():
            stage(t - delay)

    def v_copies():
        return [
            remote(vbuf, vrecv.at[d - 1], small_s.at[3 + d], small_r.at[3 + d], on_y((y + d) % SIDE))
            for d in (1, 2, 3)
        ]

    def half_copy():
        return remote(half.at[1], half.at[2], small_s.at[7], small_r.at[7], sister)

    def ring_copies(axis):
        copies = []
        for d in (1, 2, 3):
            to = on_ab((a + d) % SIDE, b) if axis == 0 else on_ab(a, (b + d) % SIDE)
            k = 7 + 3 * axis + d
            copies.append(remote(ring.at[axis, 0], ring.at[axis, d], small_s.at[k], small_r.at[k], to))
        return copies

    def back_sum():
        v = jnp.sum(back[...], axis=1, keepdims=True)
        vbuf[...] = jnp.broadcast_to(v, vbuf.shape)
        for copy in v_copies():
            copy.start()

    def back_centre():
        for copy in v_copies():
            copy.wait()
        mean = (vbuf[...] + vrecv[0] + vrecv[1] + vrecv[2]) * (1.0 / TIME)
        half[0] = back[:, :PTS] - mean
        half[1] = back[:, PTS:] - mean
        half_copy().start()

    def back_cores():
        half_copy().wait()
        ring[0, 0] = half[0] + half[2]
        for copy in ring_copies(0):
            copy.start()

    def back_first():
        for copy in ring_copies(0):
            copy.wait()
        ring[1, 0] = ring[0, 0] + ring[0, 1] + ring[0, 2] + ring[0, 3]
        for copy in ring_copies(1):
            copy.start()

    def back_second():
        for copy in ring_copies(1):
            copy.wait()
        total = ring[1, 0] + ring[1, 1] + ring[1, 2] + ring[1, 3]
        all_points = jnp.sum(counts[...].astype(F32), axis=0, keepdims=True)
        scale = 1.0 / jnp.sqrt(jnp.sum(all_points, axis=1, keepdims=True))
        proj[...] = total.T * scale

    def once(t, at, stage):
        @pl.when(t == at)
        def _():
            stage()

    ended = CLASSES - 1 + DELAYS[4]

    @pl.loop(0, max(CLASSES + DELAYS[6], ended + 5))
    def _(t):
        when(t, DELAYS[0], terms)
        when(t, DELAYS[4], spread)
        when(t, DELAYS[1], add_across)
        when(t, DELAYS[2], finish_sum)
        when(t, DELAYS[3], forward)
        when(t, DELAYS[5], turn)
        when(t, DELAYS[6], hand_over)
        when(t, DELAYS[4], project)
        once(t, ended, back_sum)
        once(t, ended + 1, back_centre)
        once(t, ended + 1, back_cores)
        once(t, ended + 2, back_first)
        once(t, ended + 3, back_second)

    for j in range(CLASSES):
        out_copy(j).wait()


def place(info, rec, proj, out, proj_out, sem):
    @pl.loop(0, SPACES)
    def _(source):
        first = jnp.clip(lax.rem(info[2 * source, 0] + info[2 * source + 1, 0], CAP), 0, CAP - 1)
        turned = lax.rem(source, SIDE) * SIDE + lax.div(source, SIDE)
        for r in range(CAP):
            at = first + r
            at = jnp.where(at >= CAP, at - CAP, at)
            odd = lax.rem(at, 2)
            tile = (odd * CLASSES + lax.div(at, 2)) * SPACES + jnp.where(odd == 0, source, turned)
            pltpu.make_async_copy(rec.at[tile], out.at[source * CAP + r], sem).start()

    proj_out[...] = proj[...]
    pltpu.make_async_copy(rec, out, sem).wait()


def local(slab, counts, owner, omega):
    names = owner.reshape(SPACES * TPD // LANES, LANES)
    counts = counts.reshape(names.shape)
    smem, vmem, hbm = (pl.BlockSpec(memory_space=m) for m in (pltpu.SMEM, pltpu.VMEM, pl.ANY))
    dma = pltpu.SemaphoreType.DMA
    piece = (PER, PIECE, LANES)
    tile = (PTS, LANES)
    rec, proj, info = pl.pallas_call(
        exchange,
        out_shape=(
            pltpu.VMEM((2, CLASSES, SIDE, SIDE) + tile, BF16),
            jax.ShapeDtypeStruct(tile, F32),
            jax.ShapeDtypeStruct(names.shape, jnp.int32),
        ),
        in_specs=[vmem, vmem, vmem, hbm],
        out_specs=(vmem, vmem, vmem),
        scratch_shapes=[
            pltpu.VMEM((8, 4 * LANES), jnp.int32),
            pltpu.SMEM((8, 4 * LANES), jnp.int32),
            pltpu.VMEM((TPD,) + tile, BF16),
            pltpu.VMEM((CLASSES, PER) + tile, BF16),
            pltpu.VMEM((CLASSES, PER) + tile, BF16),
            pltpu.VMEM(tile, BF16),
            pltpu.VMEM((2 * PTS, 2 * LANES), BF16),
            pltpu.VMEM((8, LANES), F32),
            pltpu.VMEM((3, 8, LANES), F32),
            pltpu.VMEM((CLASSES, SIDE, 2) + piece, BF16),
            pltpu.VMEM((CLASSES, 2) + piece, BF16),
            pltpu.VMEM((CLASSES, 4) + piece, BF16),
            pltpu.VMEM((CLASSES, SIDE, 2) + piece, BF16),
            pltpu.VMEM((PER + 1,) + tile, BF16),
            pltpu.VMEM((CLASSES, SIDE, SIDE) + tile, BF16),
            pltpu.VMEM((CLASSES, SIDE, SIDE) + tile, BF16),
            pltpu.VMEM((LANES, 2 * PTS), F32),
            pltpu.VMEM((LANES, LANES), F32),
            pltpu.VMEM((3, LANES, LANES), F32),
            pltpu.VMEM((3, LANES, PTS), F32),
            pltpu.VMEM((2, SIDE, LANES, PTS), F32),
            dma, dma,
            dma((CLASSES,)), dma((CLASSES,)),
            dma((14,)), dma((14,)),
            dma((CLASSES, 2)), dma((CLASSES, 2)),
            dma((CLASSES, 4)), dma((CLASSES, 4)),
            dma((CLASSES, 2)), dma((CLASSES, 2)),
            dma((CLASSES, 2)), dma((CLASSES, 2)),
            dma((CLASSES, 3)), dma((CLASSES, 3)),
            dma((CLASSES, 3)), dma((CLASSES, 3)),
            dma((CLASSES,)), dma((CLASSES,)),
        ],
        compiler_params=pltpu.CompilerParams(
            collective_id=0, has_side_effects=True, vmem_limit_bytes=46 << 20
        ),
        name="exchange",
    )(names, counts, omega, slab)
    probe_owned, projected = pl.pallas_call(
        place,
        out_shape=(
            jax.ShapeDtypeStruct((SPACES * CAP,) + tile, BF16),
            jax.ShapeDtypeStruct(tile, F32),
        ),
        in_specs=[smem, hbm, vmem],
        out_specs=(hbm, vmem),
        scratch_shapes=[dma],
        compiler_params=pltpu.CompilerParams(vmem_limit_bytes=16 << 20),
        name="place",
    )(info, rec.reshape((SPACES * CAP,) + tile), proj)
    return probe_owned, projected


def solution(mesh):
    return jax.shard_map(
        local,
        mesh=mesh,
        in_specs=(P("space", None, "tm"), P(), P(), P("tm", None)),
        out_specs=(P("space", None, None), P("tm", None)),
        check_vma=False,
    )
```
